32 devices in a mesh: dp: 16 (over z, y, core), tensor: 2 (over x).
Axes of the slice: x: 2, y: 2, z: 4, core: 2. Of those that a mesh axis runs over, the one named last changes fastest.
Arguments:
- context: bfloat16 [4096, 3072], P('dp', 'tensor'), may hold values from -6 to 6
- residual: bfloat16 [4096, 5120], P(('dp', 'tensor')), may hold values from -36 to 36
- out_weight: bfloat16 [5120, 3072], P('dp', 'tensor'), may hold values from -0.109375 to 0.109375
- norm_gain: float32 [5120], replicated, may hold values from 0.5 to 2
- normed_grad: bfloat16 [4096, 5120], P(('dp', 'tensor')), may hold values from -6 to 6
- stream_grad: bfloat16 [4096, 5120], P(('dp', 'tensor')), may hold values from -6 to 6
- sketch_in: int32 [3072, 64], P('tensor'), may hold values from -1 to 1
- sketch_out: int32 [5120, 64], replicated, may hold values from -1 to 1
- example_ids: int32 [4096], P(('dp', 'tensor')), may hold values from 0 to 15, as said below
Outputs:
- grad_hidden: bfloat16 [4096, 5120], P(('dp', 'tensor'))
- grad_context: bfloat16 [4096, 3072], P('dp', 'tensor')
- sketches: float32 [16, 4096], P('dp', 'tensor')
The draws below stay inside these ranges and needn't reach their ends.
Inputs may be any that keep to these rules, and one draw needn't show every extreme that they name: `example_ids`: each aligned block of 256 tokens belongs to one example, and every example owns exactly one such block.
All inputs are finite; a program needn't handle non-finite values.
Results may differ from the reference program's by a relative error of at most 0.0095.
Values may be sent and summed in bfloat16 or wider, within the bound.
A program may use at most 128 MiB of HBM per device.

```python
import math
import jax
import jax.numpy as jnp
from jax import lax

D = 5120
HD = 128
HQ = 24
R = 64
TOK_DEV = 256
RUN = 256
TOKENS = 4096
EXAMPLES = 16
N_TENSOR = 2


def common_base(key):
    return jnp.clip(jax.random.normal(key, (TOKENS, D), jnp.float32), -4.0, 4.0)


def draw_residual(key, part):
    base = common_base(key)
    key = jax.random.fold_in(key, 11)
    key_cols, key_rows = jax.random.split(key, 2)
    col_scale = jnp.exp(jax.random.uniform(key_cols, (D,), jnp.float32, math.log(0.3), math.log(3.0)))
    row_scale = jnp.exp(jax.random.uniform(key_rows, (TOKENS, 1), jnp.float32, math.log(0.5), math.log(2.0)))
    return (base * col_scale[None, :] * row_scale).astype(jnp.bfloat16)


def draw_normed_grad(key, part):
    base = common_base(key)
    key = jax.random.fold_in(key, 29)
    noise = jnp.clip(jax.random.normal(key, (TOKENS, D), jnp.float32), -4.0, 4.0)
    return (0.6 * base + 0.8 * noise).astype(jnp.bfloat16)


def draw_example_ids(key, part):
    key = jax.random.fold_in(key, 23)
    owners = jax.random.permutation(key, EXAMPLES)
    return jnp.repeat(owners, RUN).astype(jnp.int32)


def place_ends(entries, stream_key, low, top_value):
    spot = [jax.random.randint(jax.random.fold_in(stream_key, axis), (), 0, length) for axis, length in enumerate(entries.shape)]
    main_axis = entries.shape.index(max(entries.shape))
    neighbour = spot[:main_axis] + [(spot[main_axis] + 1) % entries.shape[main_axis]] + spot[main_axis + 1:]
    return entries.at[tuple(spot)].set(low).at[tuple(neighbour)].set(top_value)


def block_levels(stream_key, dims, pieces, low, largest):
    factor_of = 1.0
    for dim, shards_of in pieces:
        steps = jax.random.uniform(jax.random.fold_in(jax.random.fold_in(stream_key, 6), dim), (shards_of,), jnp.float32, low / len(pieces), largest / len(pieces))
        factor_of = factor_of * jnp.repeat(jnp.exp(steps), dims[dim] // shards_of).reshape((-1,) + (1,) * (len(dims) - 1 - dim))
    return factor_of


def scatter_about(stream_key, dims, spread, most, pieces=(), held_as=jnp.bfloat16):
    result = jax.random.normal(stream_key, dims, jnp.float32) * spread
    if len(pieces) > 0:
        result = block_levels(stream_key, dims, pieces, -0.22, 0.18) * result
    return jnp.clip(result, min=-most, max=most).astype(held_as)


def setup_inputs(seed: int = 0) -> dict:
    splits = jax.random.split(jax.random.key(seed), 10)
    context = scatter_about(splits[0], (TOKENS, HQ * HD), 1.0, 6.0, ((0, 16), (1, 2)))
    residual = draw_residual(jax.random.fold_in(splits[9], 71), 0)
    out_weight = scatter_about(splits[2], (D, HQ * HD), (HQ * HD) ** -0.5, 0.109375, ((0, 16), (1, 2)))
    norm_gain = jnp.clip(jnp.exp(jax.random.uniform(splits[3], (D,), jnp.float32, math.log(0.5), math.log(2.0))), 0.5, 2.0)
    normed_grad = draw_normed_grad(jax.random.fold_in(splits[9], 71), 0)
    stream_grad = scatter_about(splits[5], (TOKENS, D), 1.0, 6.0, ((0, 32),))
    sketch_in = place_ends(jax.random.randint(splits[6], (HQ * HD, R), -1, 2), jax.random.fold_in(splits[6], 1), -1, 1).astype(jnp.int32)
    sketch_out = place_ends(jax.random.randint(splits[7], (D, R), -1, 2), jax.random.fold_in(splits[7], 1), -1, 1).astype(jnp.int32)
    example_ids = draw_example_ids(jax.random.fold_in(splits[9], 71), 0)
    return {"context": context, "residual": residual, "out_weight": out_weight, "norm_gain": norm_gain, "normed_grad": normed_grad, "stream_grad": stream_grad, "sketch_in": sketch_in, "sketch_out": sketch_out, "example_ids": example_ids}


epsilon = 1e-06

def reference(context, residual, out_weight, norm_gain, normed_grad, stream_grad, sketch_in, sketch_out, example_ids):
    group_width = HQ * HD // N_TENSOR
    in_scale = 1.0 / math.sqrt(HQ * HD)
    out_scale = 1.0 / math.sqrt(D)
    in_table = sketch_in.astype(jnp.bfloat16)
    hidden = residual.astype(jnp.float32)
    in_proj = jnp.zeros((context.shape[0], R), jnp.float32)
    for group_index in range(N_TENSOR):
        lower = group_index * group_width
        context_block = context[:, lower:lower + group_width]
        weight_block = out_weight[:, lower:lower + group_width]
        head_part = lax.dot_general(context_block, weight_block, (((1,), (1,)), ((), ())), preferred_element_type=jnp.float32).astype(jnp.bfloat16)
        hidden = hidden + head_part.astype(jnp.float32)
        proj_part = (jnp.dot(context_block, in_table[lower:lower + group_width], preferred_element_type=jnp.float32) * in_scale).astype(jnp.bfloat16)
        in_proj = in_proj + proj_part.astype(jnp.float32)
    rstd = lax.rsqrt(lax.optimization_barrier(jnp.mean(hidden * hidden, axis=-1, keepdims=True)) + epsilon)
    weighted = norm_gain.astype(jnp.float32)[None, :] * normed_grad.astype(jnp.float32)
    inner = lax.optimization_barrier(jnp.mean(weighted * hidden, axis=-1, keepdims=True))
    grad_hidden = (stream_grad.astype(jnp.float32) + rstd * weighted - hidden * (rstd * rstd * rstd) * inner).astype(jnp.bfloat16)
    grad_context = jnp.dot(grad_hidden, out_weight, preferred_element_type=jnp.float32).astype(jnp.bfloat16)
    out_proj = jnp.dot(grad_hidden, sketch_out.astype(jnp.bfloat16), preferred_element_type=jnp.float32) * out_scale
    pairs = (in_proj[:, :, None] * out_proj[:, None, :]).reshape(in_proj.shape[0], R * R)
    one_hot = (example_ids[:, None] == jnp.arange(EXAMPLES, dtype=jnp.int32)[None, :]).astype(jnp.float32)
    summed = lax.dot_general(one_hot, pairs, (((0,), (0,)), ((), ())), precision=lax.Precision.HIGHEST, preferred_element_type=jnp.float32)
    sketches = summed * (1.0 / math.sqrt(TOK_DEV))
    return (grad_hidden, grad_context, sketches)
```

```python
import functools
import math

import jax
import jax.numpy as jnp
from jax import lax
from jax.experimental import pallas as pl
from jax.experimental.pallas import tpu as pltpu
from jax.sharding import PartitionSpec as P

epsilon = 1e-06
MESH = pl.DeviceIdType.MESH
f32 = jnp.float32
bf16 = jnp.bfloat16


def kernel(
    dp,
    tp,
    group,
    context_hbm,
    residual_hbm,
    weight_hbm,
    gain_ref,
    normed_hbm,
    stream_hbm,
    in_hbm,
    out_hbm,
    ids_ref,
    gh_out,
    gc_out,
    sk_out,
    weight,
    context,
    residual,
    normed,
    stream,
    in_table,
    out_table,
    part_all,
    part_in,
    hidden,
    square,
    cross,
    gh_all,
    total,
    proj_all,
    proj_in,
    sk_all,
    sk_tensor,
    sk_send,
    sk_in,
    load_sem,
    w_send,
    w_recv,
    part_send,
    part_recv,
    gh_send,
    gh_recv,
    proj_send,
    proj_recv,
    skt_send,
    skt_recv,
    skd_send,
    skd_recv,
):
    me = lax.axis_index("dp")
    t = lax.axis_index("tensor")
    lines = dp // 4
    a, b, c = me // 4, lax.rem(me // 2, 2), lax.rem(me, 2)
    rows = residual.shape[0]
    width = residual.shape[1]
    shard = weight_hbm.shape[0]
    cols = group * shard
    groups = width // cols
    in_scale = 1.0 / math.sqrt(context.shape[1] * tp)
    out_scale = 1.0 / math.sqrt(width)

    def load(k, source, target):
        return pltpu.make_async_copy(source, target, load_sem.at[k])

    def place(i):
        return pl.ds(pl.multiple_of(i * shard, shard), shard)

    def block(g):
        return pl.ds(pl.multiple_of(g * cols, cols), cols)

    loads = [
        load(0, weight_hbm, weight.at[place(me)]),
        load(1, context_hbm, context),
        load(2, in_hbm, in_table),
        load(3, residual_hbm, residual),
        load(4, normed_hbm, normed),
        load(5, stream_hbm, stream),
        load(6, out_hbm, out_table),
    ]
    for copy in loads:
        copy.start()

    barrier = pltpu.get_barrier_semaphore()

    @pl.loop(1, dp)
    def _(k):
        pl.semaphore_signal(
            barrier, inc=1, device_id=(lax.rem(me + k, dp), t), device_id_type=MESH
        )

    for k in range(1, tp):
        pl.semaphore_signal(
            barrier, inc=1, device_id=(me, lax.rem(t + k, tp)), device_id_type=MESH
        )
    pl.semaphore_wait(barrier, dp - 1 + tp - 1)

    def index(a0, b0, c0):
        return (a0 * 2 + b0) * 2 + c0

    def send_weight(i, way, to):
        return pltpu.make_async_remote_copy(
            src_ref=weight.at[place(i)],
            dst_ref=weight.at[place(i)],
            send_sem=w_send.at[way, i],
            recv_sem=w_recv.at[i],
            device_id=(to, t),
            device_id_type=MESH,
        )

    def await_weight(i):
        send_weight(i, 0, index(a, b, 1 - c)).wait_recv()

    def peer(k):
        return lax.rem(t + 1 + k, tp)

    def ways(a0, act):
        i = index(a0, b, c)

        @pl.when((a0 >= a) & (a > 0))
        def _():
            act(send_weight(i, 2, index(a - 1, b, c)))

        @pl.when((a0 <= a) & (a < lines - 1))
        def _():
            act(send_weight(i, 3, index(a + 1, b, c)))

        act(send_weight(i, 1, index(a, 1 - b, c)))
        act(send_weight(i, 0, index(a, b, 1 - c)))

    def pass_on(a0, column):
        @pl.when(column == 0)
        def _():
            @pl.when(a0 != a)
            def _():
                await_weight(index(a0, b, c))

            ways(a0, lambda copy: copy.start())

        @pl.when(column == 1)
        def _():
            i = index(a0, 1 - b, c)
            await_weight(i)
            send_weight(i, 0, index(a, b, 1 - c)).start()

    def send_part(k, g):
        return pltpu.make_async_remote_copy(
            src_ref=part_all.at[g, pl.ds(pl.multiple_of(peer(k) * rows, rows), rows)],
            dst_ref=part_in.at[tp - 2 - k, g],
            send_sem=part_send.at[k, g],
            recv_sem=part_recv.at[tp - 2 - k, g],
            device_id=(me, peer(k)),
            device_id_type=MESH,
        )

    def await_part(k, g):
        pltpu.make_async_remote_copy(
            src_ref=part_in.at[k, g],
            dst_ref=part_in.at[k, g],
            send_sem=part_send.at[k, g],
            recv_sem=part_recv.at[k, g],
            device_id=(me, peer(k)),
            device_id_type=MESH,
        ).wait_recv()

    def forward(g):
        part_all[g] = lax.dot_general(
            context[...],
            weight[block(g), :],
            (((1,), (1,)), ((), ())),
            preferred_element_type=f32,
        ).astype(bf16)
        for k in range(tp - 1):
            send_part(k, g).start()

    own_rows = pl.ds(pl.multiple_of(t * rows, rows), rows)

    def weighted_of(g):
        return gain_ref[:, block(g)] * normed[:, block(g)].astype(f32)

    def gather_stats(g):
        value = residual[:, block(g)].astype(f32) + part_all[g, own_rows, :].astype(f32)
        for k in range(tp - 1):
            await_part(k, g)
            value = value + part_in[k, g].astype(f32)
        hidden[g] = value
        square[...] += jnp.sum(value * value, axis=-1, keepdims=True)
        cross[...] += jnp.sum(value * weighted_of(g), axis=-1, keepdims=True)

    square[...] = jnp.zeros_like(square)
    cross[...] = jnp.zeros_like(cross)
    loads[0].wait()

    def send_proj(k):
        return pltpu.make_async_remote_copy(
            src_ref=proj_all.at[pl.ds(pl.multiple_of(peer(k) * rows, rows), rows)],
            dst_ref=proj_in.at[tp - 2 - k],
            send_sem=proj_send.at[k],
            recv_sem=proj_recv.at[tp - 2 - k],
            device_id=(me, peer(k)),
            device_id_type=MESH,
        )

    def event(e, distance, act):
        side, column = lax.rem(e, 2), e // 2
        a0 = a + (2 * side - 1) * (distance - column)
        there = (distance - column >= 0) & (a0 >= 0) & (a0 < lines)

        @pl.when(there & ((distance != column) | (side == 0)))
        def _():
            act(a0, column)

    def whole_chip(a0, column):
        b0 = lax.rem(b + column, 2)
        await_weight(index(a0, b0, 1 - c))

    def chip_forward(a0, column):
        whole_chip(a0, column)
        forward(a0 * 2 + lax.rem(b + column, 2))

    def chip_stats(a0, column):
        gather_stats(a0 * 2 + lax.rem(b + column, 2))

    def first_loads():
        loads[1].wait()
        loads[2].wait()
        proj_all[...] = (
            jnp.dot(context[...], in_table[...].astype(f32).astype(bf16), preferred_element_type=f32)
            * in_scale
        ).astype(bf16)
        for k in range(tp - 1):
            send_proj(k).start()
        for copy in loads[3:]:
            copy.wait()

    pass_on(a, jnp.int32(0))
    first_loads()

    @pl.loop(1, lines + 3)
    def _(s):
        @pl.loop(0, 4)
        def _(e):
            event(e, s, pass_on)

        if group == 2:

            @pl.loop(0, 4)
            def _(e):
                event(e, s - 1, chip_forward)

            @pl.loop(0, 4)
            def _(e):
                event(e, s - 2, chip_stats)

        else:

            @pl.loop(0, 4)
            def _(e):
                event(e, s - 1, whole_chip)

    if group != 2:

        @pl.loop(0, groups)
        def _(g):
            forward(g)

        @pl.loop(0, groups)
        def _(g):
            gather_stats(g)

    rstd = lax.rsqrt(square[...] * (1.0 / width) + epsilon)
    pull = rstd * rstd * rstd * (cross[...] * (1.0 / width))
    square[...] = rstd
    cross[...] = pull

    def send_gh(k, g):
        return pltpu.make_async_remote_copy(
            src_ref=gh_all.at[t, g],
            dst_ref=gh_all.at[t, g],
            send_sem=gh_send.at[k, g],
            recv_sem=gh_recv.at[tp - 2 - k, g],
            device_id=(me, peer(k)),
            device_id_type=MESH,
        )

    def await_gh(k, g):
        pltpu.make_async_remote_copy(
            src_ref=gh_all.at[peer(k), g],
            dst_ref=gh_all.at[peer(k), g],
            send_sem=gh_send.at[k, g],
            recv_sem=gh_recv.at[k, g],
            device_id=(me, peer(k)),
            device_id_type=MESH,
        ).wait_recv()

    @pl.loop(0, groups)
    def _(g):
        value = (
            stream[:, block(g)].astype(f32)
            + square[...] * weighted_of(g)
            - hidden[g] * cross[...]
        ).astype(bf16)
        gh_all[t, g] = value
        gh_out[:, block(g)] = value
        for k in range(tp - 1):
            send_gh(k, g).start()

    out_proj = (
        jnp.dot(gh_out[...], out_table[...].astype(f32).astype(bf16), preferred_element_type=f32)
        * out_scale
    )
    in_proj = proj_all[own_rows, :].astype(f32)
    for k in range(tp - 1):
        send_proj(k).wait_recv()
    for k in range(tp - 1):
        in_proj = in_proj + proj_in[k].astype(f32)
    sk_all[...] = lax.dot_general(
        in_proj,
        out_proj,
        (((0,), (0,)), ((), ())),
        precision=lax.Precision.HIGHEST,
        preferred_element_type=f32,
    )
    piece = sk_out.shape[0]

    def send_skt(k):
        return pltpu.make_async_remote_copy(
            src_ref=sk_all.at[pl.ds(pl.multiple_of(peer(k) * piece, piece), piece)],
            dst_ref=sk_tensor.at[tp - 2 - k],
            send_sem=skt_send.at[k],
            recv_sem=skt_recv.at[tp - 2 - k],
            device_id=(me, peer(k)),
            device_id_type=MESH,
        )

    for k in range(tp - 1):
        send_skt(k).start()

    def backward(row, g0):
        @pl.loop(0, groups)
        def _(g):
            g0(g)
            product = jnp.dot(gh_all[row, g], weight[block(g), :], preferred_element_type=f32)

            @pl.when(g == 0)
            def _():
                total[...] = product

            @pl.when(g > 0)
            def _():
                total[...] += product

        gc_out[pl.ds(pl.multiple_of(row * rows, rows), rows), :] = total[...].astype(bf16)

    backward(t, lambda g: None)

    summed = sk_all[pl.ds(pl.multiple_of(t * piece, piece), piece), :]
    for k in range(tp - 1):
        send_skt(k).wait_recv()
    for k in range(tp - 1):
        summed = summed + sk_tensor[k]
    summed = summed * (1.0 / math.sqrt(context.shape[0]))
    sk_out[...] = summed

    def send_skd(r):
        return pltpu.make_async_remote_copy(
            src_ref=sk_send.at[r],
            dst_ref=sk_in.at[me],
            send_sem=skd_send.at[r],
            recv_sem=skd_recv.at[me],
            device_id=(r, t),
            device_id_type=MESH,
        )

    def await_skd(r):
        pltpu.make_async_remote_copy(
            src_ref=sk_in.at[r],
            dst_ref=sk_in.at[r],
            send_sem=skd_send.at[r],
            recv_sem=skd_recv.at[r],
            device_id=(r, t),
            device_id_type=MESH,
        ).wait_recv()

    owner = jnp.broadcast_to(ids_ref[0:1, 0:1], sk_out.shape)

    @pl.loop(1, dp)
    def _(k):
        r = lax.rem(me + k, dp)
        sk_send[r] = jnp.where(owner == r, sk_out[...], 0.0)
        send_skd(r).start()

    for k in range(tp - 1):
        backward(peer(k), functools.partial(await_gh, k))

    sk_out[...] = jnp.where(owner == me, sk_out[...], 0.0)

    @pl.loop(1, dp)
    def _(k):
        r = lax.rem(me + k, dp)
        await_skd(r)
        sk_out[...] += sk_in[r]

    @pl.loop(0, lines)
    def _(a0):
        ways(a0, lambda copy: copy.wait_send())
        i = index(a0, 1 - b, c)
        send_weight(i, 0, index(a, b, 1 - c)).wait_send()

    for k in range(tp - 1):
        send_proj(k).wait_send()
        send_skt(k).wait_send()

        @pl.loop(0, groups)
        def _(g):
            send_part(k, g).wait_send()
            send_gh(k, g).wait_send()

    @pl.loop(1, dp)
    def _(k):
        send_skd(lax.rem(me + k, dp)).wait_send()


def on_device(
    context,
    residual,
    out_weight,
    norm_gain,
    normed_grad,
    stream_grad,
    sketch_in,
    sketch_out,
    example_ids,
):
    tp = lax.axis_size("tensor")
    dp = lax.axis_size("dp")
    tokens, heads = context.shape
    rows, width = residual.shape
    shard = out_weight.shape[0]
    rank = sketch_in.shape[1]
    group = 2
    while (group * shard) % 128:
        group *= 2
    cols = group * shard
    groups = width // cols
    piece = rank // tp
    hbm = pl.BlockSpec(memory_space=pl.ANY)
    vmem = pl.BlockSpec(memory_space=pltpu.VMEM)
    dma = pltpu.SemaphoreType.DMA
    flops = 4 * tokens * heads * width
    grad_hidden, grad_context, sketch = pl.pallas_call(
        functools.partial(kernel, dp, tp, group),
        out_shape=(
            jax.ShapeDtypeStruct((rows, width), bf16),
            jax.ShapeDtypeStruct((tokens, heads), bf16),
            jax.ShapeDtypeStruct((piece, rank), f32),
        ),
        in_specs=[hbm, hbm, hbm, vmem, hbm, hbm, hbm, hbm, vmem],
        out_specs=(vmem, vmem, vmem),
        scratch_shapes=[
            pltpu.VMEM((width, heads), bf16),
            pltpu.VMEM((tokens, heads), bf16),
            pltpu.VMEM((rows, width), bf16),
            pltpu.VMEM((rows, width), bf16),
            pltpu.VMEM((rows, width), bf16),
            pltpu.VMEM((heads, rank), jnp.int32),
            pltpu.VMEM((width, rank), jnp.int32),
            pltpu.VMEM((groups, tokens, cols), bf16),
            pltpu.VMEM((tp - 1, groups, rows, cols), bf16),
            pltpu.VMEM((groups, rows, cols), f32),
            pltpu.VMEM((rows, 1), f32),
            pltpu.VMEM((rows, 1), f32),
            pltpu.VMEM((tp, groups, rows, cols), bf16),
            pltpu.VMEM((rows, heads), f32),
            pltpu.VMEM((tokens, rank), bf16),
            pltpu.VMEM((tp - 1, rows, rank), bf16),
            pltpu.VMEM((rank, rank), f32),
            pltpu.VMEM((tp - 1, piece, rank), f32),
            pltpu.VMEM((dp, piece, rank), f32),
            pltpu.VMEM((dp, piece, rank), f32),
            dma((7,)),
            dma((4, dp)),
            dma((dp,)),
            dma((tp - 1, groups)),
            dma((tp - 1, groups)),
            dma((tp - 1, groups)),
            dma((tp - 1, groups)),
            dma((tp - 1,)),
            dma((tp - 1,)),
            dma((tp - 1,)),
            dma((tp - 1,)),
            dma((dp,)),
            dma((dp,)),
        ],
        compiler_params=pltpu.CompilerParams(
            collective_id=0, has_side_effects=True, vmem_limit_bytes=56 * 1024 * 1024
        ),
        cost_estimate=pl.CostEstimate(
            flops=flops, bytes_accessed=16 * 1024 * 1024, transcendentals=0
        ),
    )(
        context,
        residual,
        out_weight,
        norm_gain.reshape(1, width),
        normed_grad,
        stream_grad,
        sketch_in,
        sketch_out,
        example_ids.reshape(1, rows),
    )
    return (grad_hidden, grad_context, sketch.reshape(1, piece * rank))


def solution(mesh):
    return jax.shard_map(
        on_device,
        mesh=mesh,
        in_specs=(
            P("dp", "tensor"),
            P(("dp", "tensor"), None),
            P("dp", "tensor"),
            P(),
            P(("dp", "tensor"), None),
            P(("dp", "tensor"), None),
            P("tensor", None),
            P(),
            P(("dp", "tensor")),
        ),
        out_specs=(P(("dp", "tensor"), None), P("dp", "tensor"), P("dp", "tensor")),
        check_vma=False,
    )
```

```python
import functools
import math

import jax
import jax.numpy as jnp
from jax import lax
from jax.experimental import pallas as pl
from jax.experimental.pallas import tpu as pltpu
from jax.sharding import PartitionSpec as P

epsilon = 1e-06
MESH = pl.DeviceIdType.MESH
f32 = jnp.float32
bf16 = jnp.bfloat16


def kernel(
    dp,
    tp,
    group,
    context_hbm,
    residual_hbm,
    weight_hbm,
    gain_ref,
    normed_hbm,
    stream_hbm,
    in_hbm,
    out_hbm,
    ids_ref,
    gh_out,
    gc_out,
    sk_out,
    weight,
    context,
    residual,
    normed,
    stream,
    in_table,
    out_table,
    part_all,
    part_in,
    hidden,
    square,
    cross,
    gh_all,
    total,
    proj_all,
    proj_in,
    sk_all,
    sk_tensor,
    sk_send,
    sk_in,
    load_sem,
    w_send,
    w_recv,
    part_send,
    part_recv,
    gh_send,
    gh_recv,
    proj_send,
    proj_recv,
    skt_send,
    skt_recv,
    skd_send,
    skd_recv,
):
    me = lax.axis_index("dp")
    t = lax.axis_index("tensor")
    lines = dp // 4
    a, b, c = me // 4, lax.rem(me // 2, 2), lax.rem(me, 2)
    rows = residual.shape[0]
    width = residual.shape[1]
    shard = weight_hbm.shape[0]
    cols = group * shard
    groups = width // cols
    in_scale = 1.0 / math.sqrt(context.shape[1] * tp)
    out_scale = 1.0 / math.sqrt(width)

    def load(k, source, target):
        return pltpu.make_async_copy(source, target, load_sem.at[k])

    def place(i):
        return pl.ds(pl.multiple_of(i * shard, shard), shard)

    def block(g):
        return pl.ds(pl.multiple_of(g * cols, cols), cols)

    loads = [
        load(0, weight_hbm, weight.at[place(me)]),
        load(1, context_hbm, context),
        load(2, in_hbm, in_table),
        load(3, residual_hbm, residual),
        load(4, normed_hbm, normed),
        load(5, stream_hbm, stream),
        load(6, out_hbm, out_table),
    ]
    for copy in loads:
        copy.start()

    barrier = pltpu.get_barrier_semaphore()

    @pl.loop(1, dp)
    def _(k):
        pl.semaphore_signal(
            barrier, inc=1, device_id=(lax.rem(me + k, dp), t), device_id_type=MESH
        )

    for k in range(1, tp):
        pl.semaphore_signal(
            barrier, inc=1, device_id=(me, lax.rem(t + k, tp)), device_id_type=MESH
        )
    pl.semaphore_wait(barrier, dp - 1 + tp - 1)

    def index(a0, b0, c0):
        return (a0 * 2 + b0) * 2 + c0

    cut = shard // 32 * 16
    halves = ((0, cut), (cut, shard - cut))

    def send_weight(i, h, way, to):
        first, count = halves[h]
        where = pl.ds(pl.multiple_of(i * shard + first, 16), count)
        return pltpu.make_async_remote_copy(
            src_ref=weight.at[where],
            dst_ref=weight.at[where],
            send_sem=w_send.at[way, h, i],
            recv_sem=w_recv.at[h, i],
            device_id=(to, t),
            device_id_type=MESH,
        )

    def await_weight(i, h):
        send_weight(i, h, 0, index(a, b, 1 - c)).wait_recv()

    def peer(k):
        return lax.rem(t + 1 + k, tp)

    def crosses(a0, at, h):
        far = lax.abs(at - a0) >= 2
        end = (a0 == 0) | (a0 == lines - 1)
        return jnp.logical_not(far & end) if h == 1 else jnp.bool_(True)

    def ways(a0, column, h, act):
        b0 = lax.rem(b + column, 2)
        i = index(a0, b0, c)
        along = column == 0

        @pl.when((a0 >= a) & (a > 0) & (along | jnp.logical_not(crosses(a0, a - 1, h))))
        def _():
            act(send_weight(i, h, 2, index(a - 1, b, c)))

        @pl.when(
            (a0 <= a) & (a < lines - 1) & (along | jnp.logical_not(crosses(a0, a + 1, h)))
        )
        def _():
            act(send_weight(i, h, 3, index(a + 1, b, c)))

        @pl.when(along & crosses(a0, a, h))
        def _():
            act(send_weight(i, h, 1, index(a, 1 - b, c)))

        act(send_weight(i, h, 0, index(a, b, 1 - c)))

    def pass_on(h, a0, column):
        i = index(a0, lax.rem(b + column, 2), c)

        @pl.when((a0 != a) | (column != 0))
        def _():
            await_weight(i, h)

        ways(a0, column, h, lambda copy: copy.start())

    def send_part(k, g):
        return pltpu.make_async_remote_copy(
            src_ref=part_all.at[g, pl.ds(pl.multiple_of(peer(k) * rows, rows), rows)],
            dst_ref=part_in.at[tp - 2 - k, g],
            send_sem=part_send.at[k, g],
            recv_sem=part_recv.at[tp - 2 - k, g],
            device_id=(me, peer(k)),
            device_id_type=MESH,
        )

    def await_part(k, g):
        pltpu.make_async_remote_copy(
            src_ref=part_in.at[k, g],
            dst_ref=part_in.at[k, g],
            send_sem=part_send.at[k, g],
            recv_sem=part_recv.at[k, g],
            device_id=(me, peer(k)),
            device_id_type=MESH,
        ).wait_recv()

    def forward(g):
        part_all[g] = lax.dot_general(
            context[...],
            weight[block(g), :],
            (((1,), (1,)), ((), ())),
            preferred_element_type=f32,
        ).astype(bf16)
        for k in range(tp - 1):
            send_part(k, g).start()

    own_rows = pl.ds(pl.multiple_of(t * rows, rows), rows)

    def weighted_of(g):
        return gain_ref[:, block(g)] * normed[:, block(g)].astype(f32)

    def gather_stats(g):
        value = residual[:, block(g)].astype(f32) + part_all[g, own_rows, :].astype(f32)
        for k in range(tp - 1):
            await_part(k, g)
            value = value + part_in[k, g].astype(f32)
        hidden[g] = value
        square[...] += jnp.sum(value * value, axis=-1, keepdims=True)
        cross[...] += jnp.sum(value * weighted_of(g), axis=-1, keepdims=True)

    square[...] = jnp.zeros_like(square)
    cross[...] = jnp.zeros_like(cross)
    loads[0].wait()

    def send_proj(k):
        return pltpu.make_async_remote_copy(
            src_ref=proj_all.at[pl.ds(pl.multiple_of(peer(k) * rows, rows), rows)],
            dst_ref=proj_in.at[tp - 2 - k],
            send_sem=proj_send.at[k],
            recv_sem=proj_recv.at[tp - 2 - k],
            device_id=(me, peer(k)),
            device_id_type=MESH,
        )

    def event(e, distance, act):
        side, column = lax.rem(e, 2), e // 2
        a0 = a + (2 * side - 1) * (distance - column)
        there = (distance - column >= 0) & (a0 >= 0) & (a0 < lines)

        @pl.when(there & ((distance != column) | (side == 0)))
        def _():
            act(a0, column)

    def whole_chip(a0, column):
        b0 = lax.rem(b + column, 2)
        for h in (1, 0):
            await_weight(index(a0, b0, 1 - c), h)

    def chip_forward(a0, column):
        whole_chip(a0, column)
        forward(a0 * 2 + lax.rem(b + column, 2))

    def chip_stats(a0, column):
        gather_stats(a0 * 2 + lax.rem(b + column, 2))

    def first_loads():
        loads[1].wait()
        loads[2].wait()
        proj_all[...] = (
            lax.dot_general(
                context[...],
                in_table[...].astype(f32).astype(bf16),
                (((1,), (1,)), ((), ())),
                preferred_element_type=f32,
            )
            * in_scale
        ).astype(bf16)
        for k in range(tp - 1):
            send_proj(k).start()
        for copy in loads[3:]:
            copy.wait()

    for h in (1, 0):
        pass_on(h, a, jnp.int32(0))
    first_loads()

    @pl.loop(1, lines + 3)
    def _(s):
        for h in (1, 0):

            @pl.loop(0, 4)
            def _(e):
                event(e, s, functools.partial(pass_on, h))

        if group == 2:

            @pl.loop(0, 4)
            def _(e):
                event(e, s - 1, chip_forward)

            @pl.loop(0, 4)
            def _(e):
                event(e, s - 2, chip_stats)

        else:

            @pl.loop(0, 4)
            def _(e):
                event(e, s - 1, whole_chip)

    if group != 2:

        @pl.loop(0, groups)
        def _(g):
            forward(g)

        @pl.loop(0, groups)
        def _(g):
            gather_stats(g)

    rstd = lax.rsqrt(square[...] * (1.0 / width) + epsilon)
    pull = rstd * rstd * rstd * (cross[...] * (1.0 / width))
    square[...] = rstd
    cross[...] = pull

    def send_gh(k, g):
        return pltpu.make_async_remote_copy(
            src_ref=gh_all.at[t, g],
            dst_ref=gh_all.at[t, g],
            send_sem=gh_send.at[k, g],
            recv_sem=gh_recv.at[tp - 2 - k, g],
            device_id=(me, peer(k)),
            device_id_type=MESH,
        )

    def await_gh(k, g):
        pltpu.make_async_remote_copy(
            src_ref=gh_all.at[peer(k), g],
            dst_ref=gh_all.at[peer(k), g],
            send_sem=gh_send.at[k, g],
            recv_sem=gh_recv.at[k, g],
            device_id=(me, peer(k)),
            device_id_type=MESH,
        ).wait_recv()

    @pl.loop(0, groups)
    def _(g):
        value = (
            stream[:, block(g)].astype(f32)
            + square[...] * weighted_of(g)
            - hidden[g] * cross[...]
        ).astype(bf16)
        gh_all[t, g] = value
        gh_out[:, block(g)] = value
        for k in range(tp - 1):
            send_gh(k, g).start()

    out_proj = (
        lax.dot_general(
            gh_out[...],
            out_table[...].astype(f32).astype(bf16),
            (((1,), (1,)), ((), ())),
            preferred_element_type=f32,
        )
        * out_scale
    )
    in_proj = proj_all[own_rows, :].astype(f32)
    for k in range(tp - 1):
        send_proj(k).wait_recv()
    for k in range(tp - 1):
        in_proj = in_proj + proj_in[k].astype(f32)
    sk_all[...] = lax.dot_general(
        in_proj,
        out_proj,
        (((0,), (0,)), ((), ())),
        precision=lax.Precision.HIGHEST,
        preferred_element_type=f32,
    )
    piece = sk_out.shape[0]

    def send_skt(k):
        return pltpu.make_async_remote_copy(
            src_ref=sk_all.at[pl.ds(pl.multiple_of(peer(k) * piece, piece), piece)],
            dst_ref=sk_tensor.at[tp - 2 - k],
            send_sem=skt_send.at[k],
            recv_sem=skt_recv.at[tp - 2 - k],
            device_id=(me, peer(k)),
            device_id_type=MESH,
        )

    for k in range(tp - 1):
        send_skt(k).start()

    def backward(row, g0):
        @pl.loop(0, groups)
        def _(g):
            g0(g)
            product = jnp.dot(gh_all[row, g], weight[block(g), :], preferred_element_type=f32)

            @pl.when(g == 0)
            def _():
                total[...] = product

            @pl.when(g > 0)
            def _():
                total[...] += product

        gc_out[pl.ds(pl.multiple_of(row * rows, rows), rows), :] = total[...].astype(bf16)

    backward(t, lambda g: None)

    summed = sk_all[pl.ds(pl.multiple_of(t * piece, piece), piece), :]
    for k in range(tp - 1):
        send_skt(k).wait_recv()
    for k in range(tp - 1):
        summed = summed + sk_tensor[k]
    summed = summed * (1.0 / math.sqrt(context.shape[0]))
    sk_out[...] = summed

    def send_skd(r):
        return pltpu.make_async_remote_copy(
            src_ref=sk_send.at[r],
            dst_ref=sk_in.at[me],
            send_sem=skd_send.at[r],
            recv_sem=skd_recv.at[me],
            device_id=(r, t),
            device_id_type=MESH,
        )

    def await_skd(r):
        pltpu.make_async_remote_copy(
            src_ref=sk_in.at[r],
            dst_ref=sk_in.at[r],
            send_sem=skd_send.at[r],
            recv_sem=skd_recv.at[r],
            device_id=(r, t),
            device_id_type=MESH,
        ).wait_recv()

    owner = jnp.broadcast_to(ids_ref[0:1, 0:1], sk_out.shape)

    @pl.loop(1, dp)
    def _(k):
        r = lax.rem(me + k, dp)
        sk_send[r] = jnp.where(owner == r, sk_out[...], 0.0)
        send_skd(r).start()

    for k in range(tp - 1):
        backward(peer(k), functools.partial(await_gh, k))

    sk_out[...] = jnp.where(owner == me, sk_out[...], 0.0)

    @pl.loop(1, dp)
    def _(k):
        r = lax.rem(me + k, dp)
        await_skd(r)
        sk_out[...] += sk_in[r]

    @pl.loop(0, lines)
    def _(a0):
        for column in (0, 1):
            for h in (1, 0):
                ways(a0, jnp.int32(column), h, lambda copy: copy.wait_send())

    for k in range(tp - 1):
        send_proj(k).wait_send()
        send_skt(k).wait_send()

        @pl.loop(0, groups)
        def _(g):
            send_part(k, g).wait_send()
            send_gh(k, g).wait_send()

    @pl.loop(1, dp)
    def _(k):
        send_skd(lax.rem(me + k, dp)).wait_send()


def on_device(
    context,
    residual,
    out_weight,
    norm_gain,
    normed_grad,
    stream_grad,
    sketch_in,
    sketch_out,
    example_ids,
):
    tp = lax.axis_size("tensor")
    dp = lax.axis_size("dp")
    tokens, heads = context.shape
    rows, width = residual.shape
    shard = out_weight.shape[0]
    rank = sketch_in.shape[1]
    group = 2
    while (group * shard) % 128:
        group *= 2
    cols = group * shard
    groups = width // cols
    piece = rank // tp
    hbm = pl.BlockSpec(memory_space=pl.ANY)
    vmem = pl.BlockSpec(memory_space=pltpu.VMEM)
    dma = pltpu.SemaphoreType.DMA
    flops = 4 * tokens * heads * width
    grad_hidden, grad_context, sketch = pl.pallas_call(
        functools.partial(kernel, dp, tp, group),
        out_shape=(
            jax.ShapeDtypeStruct((rows, width), bf16),
            jax.ShapeDtypeStruct((tokens, heads), bf16),
            jax.ShapeDtypeStruct((piece, rank), f32),
        ),
        in_specs=[hbm, hbm, hbm, vmem, hbm, hbm, hbm, hbm, vmem],
        out_specs=(vmem, vmem, vmem),
        scratch_shapes=[
            pltpu.VMEM((width, heads), bf16),
            pltpu.VMEM((tokens, heads), bf16),
            pltpu.VMEM((rows, width), bf16),
            pltpu.VMEM((rows, width), bf16),
            pltpu.VMEM((rows, width), bf16),
            pltpu.VMEM((rank, heads), jnp.int32),
            pltpu.VMEM((rank, width), jnp.int32),
            pltpu.VMEM((groups, tokens, cols), bf16),
            pltpu.VMEM((tp - 1, groups, rows, cols), bf16),
            pltpu.VMEM((groups, rows, cols), f32),
            pltpu.VMEM((rows, 1), f32),
            pltpu.VMEM((rows, 1), f32),
            pltpu.VMEM((tp, groups, rows, cols), bf16),
            pltpu.VMEM((rows, heads), f32),
            pltpu.VMEM((tokens, rank), bf16),
            pltpu.VMEM((tp - 1, rows, rank), bf16),
            pltpu.VMEM((rank, rank), f32),
            pltpu.VMEM((tp - 1, piece, rank), f32),
            pltpu.VMEM((dp, piece, rank), f32),
            pltpu.VMEM((dp, piece, rank), f32),
            dma((7,)),
            dma((4, 2, dp)),
            dma((2, dp)),
            dma((tp - 1, groups)),
            dma((tp - 1, groups)),
            dma((tp - 1, groups)),
            dma((tp - 1, groups)),
            dma((tp - 1,)),
            dma((tp - 1,)),
            dma((tp - 1,)),
            dma((tp - 1,)),
            dma((dp,)),
            dma((dp,)),
        ],
        compiler_params=pltpu.CompilerParams(
            collective_id=0, has_side_effects=True, vmem_limit_bytes=56 * 1024 * 1024
        ),
        cost_estimate=pl.CostEstimate(
            flops=flops, bytes_accessed=16 * 1024 * 1024, transcendentals=0
        ),
    )(
        context,
        residual,
        out_weight,
        norm_gain.reshape(1, width),
        normed_grad,
        stream_grad,
        sketch_in.T,
        sketch_out.T,
        example_ids.reshape(1, rows),
    )
    return (grad_hidden, grad_context, sketch.reshape(1, piece * rank))


def solution(mesh):
    return jax.shard_map(
        on_device,
        mesh=mesh,
        in_specs=(
            P("dp", "tensor"),
            P(("dp", "tensor"), None),
            P("dp", "tensor"),
            P(),
            P(("dp", "tensor"), None),
            P(("dp", "tensor"), None),
            P("tensor", None),
            P(),
            P(("dp", "tensor")),
        ),
        out_specs=(P(("dp", "tensor"), None), P("dp", "tensor"), P("dp", "tensor")),
        check_vma=False,
    )
```

```python
import functools
import math

import jax
import jax.numpy as jnp
from jax import lax
from jax.experimental import pallas as pl
from jax.experimental.pallas import tpu as pltpu
from jax.sharding import PartitionSpec as P

epsilon = 1e-06
MESH = pl.DeviceIdType.MESH
f32 = jnp.float32
bf16 = jnp.bfloat16


def kernel(
    dp,
    tp,
    group,
    context_hbm,
    residual_hbm,
    weight_hbm,
    gain_ref,
    normed_hbm,
    stream_hbm,
    in_hbm,
    out_hbm,
    ids_ref,
    gh_out,
    gc_out,
    sk_out,
    weight,
    context,
    residual,
    normed,
    stream,
    in_table,
    out_table,
    part_all,
    part_in,
    hidden,
    square,
    cross,
    gh_all,
    total,
    proj_all,
    proj_in,
    sk_all,
    sk_tensor,
    sk_send,
    sk_in,
    load_sem,
    w_send,
    w_recv,
    part_send,
    part_recv,
    gh_send,
    gh_recv,
    proj_send,
    proj_recv,
    skt_send,
    skt_recv,
    skd_send,
    skd_recv,
    early_stream,
    early_normed,
    early_hidden,
    hidden_send,
    stat_send,
    stat_in,
    early_sent,
    early_recv,
    stat_sent,
    stat_recv,
):
    me = lax.axis_index("dp")
    t = lax.axis_index("tensor")
    lines = dp // 4
    a, b, c = me // 4, lax.rem(me // 2, 2), lax.rem(me, 2)
    rows = residual.shape[0]
    width = residual.shape[1]
    shard = weight_hbm.shape[0]
    cols = group * shard
    groups = width // cols
    early = group == 2 and tp > 1
    in_scale = 1.0 / math.sqrt(context.shape[1] * tp)
    out_scale = 1.0 / math.sqrt(width)

    def load(k, source, target):
        return pltpu.make_async_copy(source, target, load_sem.at[k])

    def place(i):
        return pl.ds(pl.multiple_of(i * shard, shard), shard)

    def block(g):
        return pl.ds(pl.multiple_of(g * cols, cols), cols)

    loads = [
        load(0, weight_hbm, weight.at[place(me)]),
        load(1, context_hbm, context),
        load(2, in_hbm, in_table),
        load(3, residual_hbm, residual),
        load(4, normed_hbm, normed),
        load(5, stream_hbm, stream),
        load(6, out_hbm, out_table),
    ]
    for copy in loads:
        copy.start()

    barrier = pltpu.get_barrier_semaphore()

    @pl.loop(1, dp)
    def _(k):
        pl.semaphore_signal(
            barrier, inc=1, device_id=(lax.rem(me + k, dp), t), device_id_type=MESH
        )

    for k in range(1, tp):
        pl.semaphore_signal(
            barrier, inc=1, device_id=(me, lax.rem(t + k, tp)), device_id_type=MESH
        )
    pl.semaphore_wait(barrier, dp - 1 + tp - 1)

    def index(a0, b0, c0):
        return (a0 * 2 + b0) * 2 + c0

    cut = shard // 32 * 16
    halves = ((0, cut), (cut, shard - cut))

    def send_weight(i, h, way, to):
        first, count = halves[h]
        where = pl.ds(pl.multiple_of(i * shard + first, 16), count)
        return pltpu.make_async_remote_copy(
            src_ref=weight.at[where],
            dst_ref=weight.at[where],
            send_sem=w_send.at[way, h, i],
            recv_sem=w_recv.at[h, i],
            device_id=(to, t),
            device_id_type=MESH,
        )

    def await_weight(i, h):
        send_weight(i, h, 0, index(a, b, 1 - c)).wait_recv()

    def peer(k):
        return lax.rem(t + 1 + k, tp)

    def crosses(a0, at, h):
        far = lax.abs(at - a0) >= 2
        end = (a0 == 0) | (a0 == lines - 1)
        return jnp.logical_not(far & end) if h == 1 else jnp.bool_(True)

    def ways(a0, column, h, act):
        b0 = lax.rem(b + column, 2)
        i = index(a0, b0, c)
        along = column == 0

        @pl.when((a0 >= a) & (a > 0) & (along | jnp.logical_not(crosses(a0, a - 1, h))))
        def _():
            act(send_weight(i, h, 2, index(a - 1, b, c)))

        @pl.when(
            (a0 <= a) & (a < lines - 1) & (along | jnp.logical_not(crosses(a0, a + 1, h)))
        )
        def _():
            act(send_weight(i, h, 3, index(a + 1, b, c)))

        @pl.when(along & crosses(a0, a, h))
        def _():
            act(send_weight(i, h, 1, index(a, 1 - b, c)))

        act(send_weight(i, h, 0, index(a, b, 1 - c)))

    def pass_on(h, a0, column):
        i = index(a0, lax.rem(b + column, 2), c)

        @pl.when((a0 != a) | (column != 0))
        def _():
            await_weight(i, h)

        ways(a0, column, h, lambda copy: copy.start())

    def send_part(k, g):
        return pltpu.make_async_remote_copy(
            src_ref=part_all.at[g, pl.ds(pl.multiple_of(peer(k) * rows, rows), rows)],
            dst_ref=part_in.at[tp - 2 - k, g],
            send_sem=part_send.at[k, g],
            recv_sem=part_recv.at[tp - 2 - k, g],
            device_id=(me, peer(k)),
            device_id_type=MESH,
        )

    def await_part(k, g):
        pltpu.make_async_remote_copy(
            src_ref=part_in.at[k, g],
            dst_ref=part_in.at[k, g],
            send_sem=part_send.at[k, g],
            recv_sem=part_recv.at[k, g],
            device_id=(me, peer(k)),
            device_id_type=MESH,
        ).wait_recv()

    def forward(g):
        part_all[g] = lax.dot_general(
            context[...],
            weight[block(g), :],
            (((1,), (1,)), ((), ())),
            preferred_element_type=f32,
        ).astype(bf16)
        for k in range(tp - 1):
            send_part(k, g).start()

    own_rows = pl.ds(pl.multiple_of(t * rows, rows), rows)

    def weighted_of(g):
        return gain_ref[:, block(g)] * normed[:, block(g)].astype(f32)

    def gather_stats(g):
        value = residual[:, block(g)].astype(f32) + part_all[g, own_rows, :].astype(f32)
        for k in range(tp - 1):
            await_part(k, g)
            value = value + part_in[k, g].astype(f32)
        hidden[g] = value
        square[...] += jnp.sum(value * value, axis=-1, keepdims=True)
        cross[...] += jnp.sum(value * weighted_of(g), axis=-1, keepdims=True)

    def ship(n, k, j):
        source = (
            stream.at[:, block(2 * j + b)],
            normed.at[:, block(2 * j + b)],
            hidden_send.at[j],
        )[n]
        target = (early_stream, early_normed, early_hidden)[n]
        return pltpu.make_async_remote_copy(
            src_ref=source,
            dst_ref=target.at[tp - 2 - k, j],
            send_sem=early_sent.at[n, k, j],
            recv_sem=early_recv.at[n, tp - 2 - k, j],
            device_id=(me, peer(k)),
            device_id_type=MESH,
        )

    def await_ship(n, k, j):
        target = (early_stream, early_normed, early_hidden)[n]
        pltpu.make_async_remote_copy(
            src_ref=target.at[k, j],
            dst_ref=target.at[k, j],
            send_sem=early_sent.at[n, k, j],
            recv_sem=early_recv.at[n, k, j],
            device_id=(me, peer(k)),
            device_id_type=MESH,
        ).wait_recv()

    def send_stat(k):
        return pltpu.make_async_remote_copy(
            src_ref=stat_send,
            dst_ref=stat_in.at[tp - 2 - k],
            send_sem=stat_sent.at[k],
            recv_sem=stat_recv.at[tp - 2 - k],
            device_id=(me, peer(k)),
            device_id_type=MESH,
        )

    square[...] = jnp.zeros_like(square)
    cross[...] = jnp.zeros_like(cross)
    loads[0].wait()

    def send_proj(k):
        return pltpu.make_async_remote_copy(
            src_ref=proj_all.at[pl.ds(pl.multiple_of(peer(k) * rows, rows), rows)],
            dst_ref=proj_in.at[tp - 2 - k],
            send_sem=proj_send.at[k],
            recv_sem=proj_recv.at[tp - 2 - k],
            device_id=(me, peer(k)),
            device_id_type=MESH,
        )

    def event(e, distance, act):
        side, column = lax.rem(e, 2), e // 2
        a0 = a + (2 * side - 1) * (distance - column)
        there = (distance - column >= 0) & (a0 >= 0) & (a0 < lines)

        @pl.when(there & ((distance != column) | (side == 0)))
        def _():
            act(a0, column)

    def whole_chip(a0, column):
        b0 = lax.rem(b + column, 2)
        for h in (1, 0):
            await_weight(index(a0, b0, 1 - c), h)

    def chip_forward(a0, column):
        whole_chip(a0, column)
        forward(a0 * 2 + lax.rem(b + column, 2))

    def chip_stats(a0, column):
        g = a0 * 2 + lax.rem(b + column, 2)
        gather_stats(g)
        if early:

            @pl.when(column == 0)
            def _():
                hidden_send[a0] = hidden[g].astype(bf16)
                for k in range(tp - 1):
                    ship(2, k, a0).start()

    def first_loads():
        loads[1].wait()
        loads[2].wait()
        proj_all[...] = (
            lax.dot_general(
                context[...],
                in_table[...].astype(f32).astype(bf16),
                (((1,), (1,)), ((), ())),
                preferred_element_type=f32,
            )
            * in_scale
        ).astype(bf16)
        for k in range(tp - 1):
            send_proj(k).start()
        for copy in loads[3:]:
            copy.wait()
        if early:

            @pl.loop(0, lines)
            def _(j):
                for k in range(tp - 1):
                    ship(0, k, j).start()
                    ship(1, k, j).start()

    for h in (1, 0):
        pass_on(h, a, jnp.int32(0))
    first_loads()

    @pl.loop(1, lines + 3)
    def _(s):
        for h in (1, 0):

            @pl.loop(0, 4)
            def _(e):
                event(e, s, functools.partial(pass_on, h))

        if group == 2:

            @pl.loop(0, 4)
            def _(e):
                event(e, s - 1, chip_forward)

            @pl.loop(0, 4)
            def _(e):
                event(e, s - 2, chip_stats)

        else:

            @pl.loop(0, 4)
            def _(e):
                event(e, s - 1, whole_chip)

    if group != 2:

        @pl.loop(0, groups)
        def _(g):
            forward(g)

        @pl.loop(0, groups)
        def _(g):
            gather_stats(g)

    rstd = lax.rsqrt(square[...] * (1.0 / width) + epsilon)
    pull = rstd * rstd * rstd * (cross[...] * (1.0 / width))
    square[...] = rstd
    cross[...] = pull
    if early:
        lane = lax.broadcasted_iota(jnp.int32, (rows, 128), 1)
        stat_send[...] = jnp.where(lane < 64, rstd, pull)
        for k in range(tp - 1):
            send_stat(k).start()

    def send_gh(k, g):
        return pltpu.make_async_remote_copy(
            src_ref=gh_all.at[t, g],
            dst_ref=gh_all.at[t, g],
            send_sem=gh_send.at[k, g],
            recv_sem=gh_recv.at[tp - 2 - k, g],
            device_id=(me, peer(k)),
            device_id_type=MESH,
        )

    def await_gh(k, g):
        pltpu.make_async_remote_copy(
            src_ref=gh_all.at[peer(k), g],
            dst_ref=gh_all.at[peer(k), g],
            send_sem=gh_send.at[k, g],
            recv_sem=gh_recv.at[k, g],
            device_id=(me, peer(k)),
            device_id_type=MESH,
        ).wait_recv()

    def own_grad(g):
        value = (
            stream[:, block(g)].astype(f32)
            + square[...] * weighted_of(g)
            - hidden[g] * cross[...]
        ).astype(bf16)
        gh_all[t, g] = value
        gh_out[:, block(g)] = value

    def sent(act):
        @pl.loop(0, lines if early else groups)
        def _(j):
            act(2 * j + 1 - b if early else j)

    def own_and_send(g):
        own_grad(g)
        for k in range(tp - 1):
            send_gh(k, g).start()

    sent(own_and_send)
    if early:

        @pl.loop(0, lines)
        def _(j):
            own_grad(2 * j + b)

    out_proj = (
        lax.dot_general(
            gh_out[...],
            out_table[...].astype(f32).astype(bf16),
            (((1,), (1,)), ((), ())),
            preferred_element_type=f32,
        )
        * out_scale
    )
    in_proj = proj_all[own_rows, :].astype(f32)
    for k in range(tp - 1):
        send_proj(k).wait_recv()
    for k in range(tp - 1):
        in_proj = in_proj + proj_in[k].astype(f32)
    sk_all[...] = lax.dot_general(
        in_proj,
        out_proj,
        (((0,), (0,)), ((), ())),
        precision=lax.Precision.HIGHEST,
        preferred_element_type=f32,
    )
    piece = sk_out.shape[0]

    def send_skt(k):
        return pltpu.make_async_remote_copy(
            src_ref=sk_all.at[pl.ds(pl.multiple_of(peer(k) * piece, piece), piece)],
            dst_ref=sk_tensor.at[tp - 2 - k],
            send_sem=skt_send.at[k],
            recv_sem=skt_recv.at[tp - 2 - k],
            device_id=(me, peer(k)),
            device_id_type=MESH,
        )

    for k in range(tp - 1):
        send_skt(k).start()

    def add(row, g):
        total[...] += jnp.dot(gh_all[row, g], weight[block(g), :], preferred_element_type=f32)

    def finish(row):
        gc_out[pl.ds(pl.multiple_of(row * rows, rows), rows), :] = total[...].astype(bf16)

    total[...] = jnp.zeros_like(total)

    @pl.loop(0, groups)
    def _(g):
        add(t, g)

    finish(t)

    summed = sk_all[pl.ds(pl.multiple_of(t * piece, piece), piece), :]
    for k in range(tp - 1):
        send_skt(k).wait_recv()
    for k in range(tp - 1):
        summed = summed + sk_tensor[k]
    summed = summed * (1.0 / math.sqrt(context.shape[0]))
    sk_out[...] = summed

    def send_skd(r):
        return pltpu.make_async_remote_copy(
            src_ref=sk_send.at[r],
            dst_ref=sk_in.at[me],
            send_sem=skd_send.at[r],
            recv_sem=skd_recv.at[me],
            device_id=(r, t),
            device_id_type=MESH,
        )

    def await_skd(r):
        pltpu.make_async_remote_copy(
            src_ref=sk_in.at[r],
            dst_ref=sk_in.at[r],
            send_sem=skd_send.at[r],
            recv_sem=skd_recv.at[r],
            device_id=(r, t),
            device_id_type=MESH,
        ).wait_recv()

    owner = jnp.broadcast_to(ids_ref[0:1, 0:1], sk_out.shape)

    @pl.loop(1, dp)
    def _(k):
        r = lax.rem(me + k, dp)
        sk_send[r] = jnp.where(owner == r, sk_out[...], 0.0)
        send_skd(r).start()

    for k in range(tp - 1):
        total[...] = jnp.zeros_like(total)
        if early:
            send_stat(tp - 2 - k).wait_recv()

            @pl.loop(0, lines)
            def _(j):
                g = 2 * j + b
                for n in range(3):
                    await_ship(n, k, j)
                gh_all[peer(k), g] = (
                    early_stream[k, j].astype(f32)
                    + stat_in[k, :, 0:1] * (gain_ref[:, block(g)] * early_normed[k, j].astype(f32))
                    - early_hidden[k, j].astype(f32) * stat_in[k, :, 64:65]
                ).astype(bf16)
                add(peer(k), g)

        def arrived(g):
            await_gh(k, g)
            add(peer(k), g)

        sent(arrived)
        finish(peer(k))

    sk_out[...] = jnp.where(owner == me, sk_out[...], 0.0)

    @pl.loop(1, dp)
    def _(k):
        r = lax.rem(me + k, dp)
        await_skd(r)
        sk_out[...] += sk_in[r]

    @pl.loop(0, lines)
    def _(a0):
        for column in (0, 1):
            for h in (1, 0):
                ways(a0, jnp.int32(column), h, lambda copy: copy.wait_send())

    for k in range(tp - 1):
        send_proj(k).wait_send()
        send_skt(k).wait_send()

        @pl.loop(0, groups)
        def _(g):
            send_part(k, g).wait_send()

        sent(lambda g: send_gh(k, g).wait_send())
        if early:
            send_stat(k).wait_send()

            @pl.loop(0, lines)
            def _(j):
                for n in range(3):
                    ship(n, k, j).wait_send()

    @pl.loop(1, dp)
    def _(k):
        send_skd(lax.rem(me + k, dp)).wait_send()


def on_device(
    context,
    residual,
    out_weight,
    norm_gain,
    normed_grad,
    stream_grad,
    sketch_in,
    sketch_out,
    example_ids,
):
    tp = lax.axis_size("tensor")
    dp = lax.axis_size("dp")
    tokens, heads = context.shape
    rows, width = residual.shape
    shard = out_weight.shape[0]
    rank = sketch_in.shape[1]
    group = 2
    while (group * shard) % 128:
        group *= 2
    cols = group * shard
    groups = width // cols
    early = (dp // 4, rows, cols) if group == 2 else (1, 16, 128)
    piece = rank // tp
    hbm = pl.BlockSpec(memory_space=pl.ANY)
    vmem = pl.BlockSpec(memory_space=pltpu.VMEM)
    dma = pltpu.SemaphoreType.DMA
    flops = 4 * tokens * heads * width
    grad_hidden, grad_context, sketch = pl.pallas_call(
        functools.partial(kernel, dp, tp, group),
        out_shape=(
            jax.ShapeDtypeStruct((rows, width), bf16),
            jax.ShapeDtypeStruct((tokens, heads), bf16),
            jax.ShapeDtypeStruct((piece, rank), f32),
        ),
        in_specs=[hbm, hbm, hbm, vmem, hbm, hbm, hbm, hbm, vmem],
        out_specs=(vmem, vmem, vmem),
        scratch_shapes=[
            pltpu.VMEM((width, heads), bf16),
            pltpu.VMEM((tokens, heads), bf16),
            pltpu.VMEM((rows, width), bf16),
            pltpu.VMEM((rows, width), bf16),
            pltpu.VMEM((rows, width), bf16),
            pltpu.VMEM((rank, heads), jnp.int32),
            pltpu.VMEM((rank, width), jnp.int32),
            pltpu.VMEM((groups, tokens, cols), bf16),
            pltpu.VMEM((tp - 1, groups, rows, cols), bf16),
            pltpu.VMEM((groups, rows, cols), f32),
            pltpu.VMEM((rows, 1), f32),
            pltpu.VMEM((rows, 1), f32),
            pltpu.VMEM((tp, groups, rows, cols), bf16),
            pltpu.VMEM((rows, heads), f32),
            pltpu.VMEM((tokens, rank), bf16),
            pltpu.VMEM((tp - 1, rows, rank), bf16),
            pltpu.VMEM((rank, rank), f32),
            pltpu.VMEM((tp - 1, piece, rank), f32),
            pltpu.VMEM((dp, piece, rank), f32),
            pltpu.VMEM((dp, piece, rank), f32),
            dma((7,)),
            dma((4, 2, dp)),
            dma((2, dp)),
            dma((tp - 1, groups)),
            dma((tp - 1, groups)),
            dma((tp - 1, groups)),
            dma((tp - 1, groups)),
            dma((tp - 1,)),
            dma((tp - 1,)),
            dma((tp - 1,)),
            dma((tp - 1,)),
            dma((dp,)),
            dma((dp,)),
            pltpu.VMEM((tp - 1,) + early, bf16),
            pltpu.VMEM((tp - 1,) + early, bf16),
            pltpu.VMEM((tp - 1,) + early, bf16),
            pltpu.VMEM(early, bf16),
            pltpu.VMEM((rows, 128), f32),
            pltpu.VMEM((tp - 1, rows, 128), f32),
            dma((3, tp - 1, early[0])),
            dma((3, tp - 1, early[0])),
            dma((tp - 1,)),
            dma((tp - 1,)),
        ],
        compiler_params=pltpu.CompilerParams(
            collective_id=0, has_side_effects=True, vmem_limit_bytes=56 * 1024 * 1024
        ),
        cost_estimate=pl.CostEstimate(
            flops=flops, bytes_accessed=16 * 1024 * 1024, transcendentals=0
        ),
    )(
        context,
        residual,
        out_weight,
        norm_gain.reshape(1, width),
        normed_grad,
        stream_grad,
        sketch_in.T,
        sketch_out.T,
        example_ids.reshape(1, rows),
    )
    return (grad_hidden, grad_context, sketch.reshape(1, piece * rank))


def solution(mesh):
    return jax.shard_map(
        on_device,
        mesh=mesh,
        in_specs=(
            P("dp", "tensor"),
            P(("dp", "tensor"), None),
            P("dp", "tensor"),
            P(),
            P(("dp", "tensor"), None),
            P(("dp", "tensor"), None),
            P("tensor", None),
            P(),
            P(("dp", "tensor")),
        ),
        out_specs=(P(("dp", "tensor"), None), P("dp", "tensor"), P("dp", "tensor")),
        check_vma=False,
    )
```

```python
import functools
import math

import jax
import jax.numpy as jnp
from jax import lax
from jax.experimental import pallas as pl
from jax.experimental.pallas import tpu as pltpu
from jax.sharding import PartitionSpec as P

epsilon = 1e-06
MESH = pl.DeviceIdType.MESH
f32 = jnp.float32
bf16 = jnp.bfloat16


def kernel(
    dp,
    tp,
    group,
    context_hbm,
    residual_hbm,
    weight_hbm,
    gain_ref,
    normed_hbm,
    stream_hbm,
    in_hbm,
    out_hbm,
    ids_ref,
    gh_out,
    gc_out,
    sk_out,
    weight,
    context,
    residual,
    normed,
    stream,
    in_table,
    out_table,
    part_all,
    part_in,
    hidden,
    square,
    cross,
    gh_all,
    total,
    proj_all,
    proj_in,
    sk_all,
    sk_tensor,
    sk_send,
    sk_in,
    load_sem,
    w_send,
    w_recv,
    part_send,
    part_recv,
    gh_send,
    gh_recv,
    proj_send,
    proj_recv,
    skt_send,
    skt_recv,
    skd_send,
    skd_recv,
    early_stream,
    early_normed,
    early_hidden,
    hidden_send,
    stat_send,
    stat_in,
    early_sent,
    early_recv,
    stat_sent,
    stat_recv,
):
    me = lax.axis_index("dp")
    t = lax.axis_index("tensor")
    lines = dp // 4
    a, b, c = me // 4, lax.rem(me // 2, 2), lax.rem(me, 2)
    rows = residual.shape[0]
    width = residual.shape[1]
    shard = weight_hbm.shape[0]
    cols = group * shard
    groups = width // cols
    early = group == 2 and tp > 1
    in_scale = 1.0 / math.sqrt(context.shape[1] * tp)
    out_scale = 1.0 / math.sqrt(width)

    def load(k, source, target):
        return pltpu.make_async_copy(source, target, load_sem.at[k])

    def place(i):
        return pl.ds(pl.multiple_of(i * shard, shard), shard)

    def block(g):
        return pl.ds(pl.multiple_of(g * cols, cols), cols)

    loads = [
        load(0, weight_hbm, weight.at[place(me)]),
        load(1, context_hbm, context),
        load(2, in_hbm, in_table),
        load(3, residual_hbm, residual),
        load(4, normed_hbm, normed),
        load(5, stream_hbm, stream),
        load(6, out_hbm, out_table),
    ]
    for copy in loads:
        copy.start()

    barrier = pltpu.get_barrier_semaphore()

    @pl.loop(1, dp)
    def _(k):
        pl.semaphore_signal(
            barrier, inc=1, device_id=(lax.rem(me + k, dp), t), device_id_type=MESH
        )

    for k in range(1, tp):
        pl.semaphore_signal(
            barrier, inc=1, device_id=(me, lax.rem(t + k, tp)), device_id_type=MESH
        )
    pl.semaphore_wait(barrier, dp - 1 + tp - 1)

    def index(a0, b0, c0):
        return (a0 * 2 + b0) * 2 + c0

    cut = shard // 32 * 16
    halves = ((0, cut), (cut, shard - cut))

    def send_weight(i, h, way, to):
        first, count = halves[h]
        where = pl.ds(pl.multiple_of(i * shard + first, 16), count)
        return pltpu.make_async_remote_copy(
            src_ref=weight.at[where],
            dst_ref=weight.at[where],
            send_sem=w_send.at[way, h, i],
            recv_sem=w_recv.at[h, i],
            device_id=(to, t),
            device_id_type=MESH,
        )

    def await_weight(i, h):
        send_weight(i, h, 0, index(a, b, 1 - c)).wait_recv()

    def peer(k):
        return lax.rem(t + 1 + k, tp)

    def crosses(a0, at, h):
        far = lax.abs(at - a0) >= 2
        end = (a0 == 0) | (a0 == lines - 1)
        return jnp.logical_not(far & end) if h == 1 else jnp.bool_(True)

    def ways(a0, column, h, act):
        b0 = lax.rem(b + column, 2)
        i = index(a0, b0, c)
        along = column == 0

        @pl.when((a0 >= a) & (a > 0) & (along | jnp.logical_not(crosses(a0, a - 1, h))))
        def _():
            act(send_weight(i, h, 2, index(a - 1, b, c)))

        @pl.when(
            (a0 <= a) & (a < lines - 1) & (along | jnp.logical_not(crosses(a0, a + 1, h)))
        )
        def _():
            act(send_weight(i, h, 3, index(a + 1, b, c)))

        @pl.when(along & crosses(a0, a, h))
        def _():
            act(send_weight(i, h, 1, index(a, 1 - b, c)))

        act(send_weight(i, h, 0, index(a, b, 1 - c)))

    def pass_on(h, a0, column):
        i = index(a0, lax.rem(b + column, 2), c)

        @pl.when((a0 != a) | (column != 0))
        def _():
            await_weight(i, h)

        ways(a0, column, h, lambda copy: copy.start())

    def send_part(k, g):
        return pltpu.make_async_remote_copy(
            src_ref=part_all.at[g, pl.ds(pl.multiple_of(peer(k) * rows, rows), rows)],
            dst_ref=part_in.at[tp - 2 - k, g],
            send_sem=part_send.at[k, g],
            recv_sem=part_recv.at[tp - 2 - k, g],
            device_id=(me, peer(k)),
            device_id_type=MESH,
        )

    def await_part(k, g):
        pltpu.make_async_remote_copy(
            src_ref=part_in.at[k, g],
            dst_ref=part_in.at[k, g],
            send_sem=part_send.at[k, g],
            recv_sem=part_recv.at[k, g],
            device_id=(me, peer(k)),
            device_id_type=MESH,
        ).wait_recv()

    def forward(g):
        part_all[g] = lax.dot_general(
            context[...],
            weight[block(g), :],
            (((1,), (1,)), ((), ())),
            preferred_element_type=f32,
        ).astype(bf16)
        for k in range(tp - 1):
            send_part(k, g).start()

    own_rows = pl.ds(pl.multiple_of(t * rows, rows), rows)

    def weighted_of(g):
        return gain_ref[:, block(g)] * normed[:, block(g)].astype(f32)

    def gather_stats(g):
        value = residual[:, block(g)].astype(f32) + part_all[g, own_rows, :].astype(f32)
        for k in range(tp - 1):
            await_part(k, g)
            value = value + part_in[k, g].astype(f32)
        hidden[g] = value
        square[...] += jnp.sum(value * value, axis=-1, keepdims=True)
        cross[...] += jnp.sum(value * weighted_of(g), axis=-1, keepdims=True)

    def ship(n, k, j):
        source = (
            stream.at[:, block(2 * j + b)],
            normed.at[:, block(2 * j + b)],
            hidden_send.at[j],
        )[n]
        target = (early_stream, early_normed, early_hidden)[n]
        return pltpu.make_async_remote_copy(
            src_ref=source,
            dst_ref=target.at[tp - 2 - k, j],
            send_sem=early_sent.at[n, k, j],
            recv_sem=early_recv.at[n, tp - 2 - k, j],
            device_id=(me, peer(k)),
            device_id_type=MESH,
        )

    def await_ship(n, k, j):
        target = (early_stream, early_normed, early_hidden)[n]
        pltpu.make_async_remote_copy(
            src_ref=target.at[k, j],
            dst_ref=target.at[k, j],
            send_sem=early_sent.at[n, k, j],
            recv_sem=early_recv.at[n, k, j],
            device_id=(me, peer(k)),
            device_id_type=MESH,
        ).wait_recv()

    def send_stat(k):
        return pltpu.make_async_remote_copy(
            src_ref=stat_send,
            dst_ref=stat_in.at[tp - 2 - k],
            send_sem=stat_sent.at[k],
            recv_sem=stat_recv.at[tp - 2 - k],
            device_id=(me, peer(k)),
            device_id_type=MESH,
        )

    square[...] = jnp.zeros_like(square)
    cross[...] = jnp.zeros_like(cross)
    loads[0].wait()

    def send_proj(k):
        return pltpu.make_async_remote_copy(
            src_ref=proj_all.at[pl.ds(pl.multiple_of(peer(k) * rows, rows), rows)],
            dst_ref=proj_in.at[tp - 2 - k],
            send_sem=proj_send.at[k],
            recv_sem=proj_recv.at[tp - 2 - k],
            device_id=(me, peer(k)),
            device_id_type=MESH,
        )

    def event(e, distance, act):
        side, column = lax.rem(e, 2), e // 2
        a0 = a + (2 * side - 1) * (distance - column)
        there = (distance - column >= 0) & (a0 >= 0) & (a0 < lines)

        @pl.when(there & ((distance != column) | (side == 0)))
        def _():
            act(a0, column)

    def whole_chip(a0, column):
        b0 = lax.rem(b + column, 2)
        for h in (1, 0):
            await_weight(index(a0, b0, 1 - c), h)

    def chip_forward(a0, column):
        whole_chip(a0, column)
        forward(a0 * 2 + lax.rem(b + column, 2))

    def chip_stats(a0, column):
        g = a0 * 2 + lax.rem(b + column, 2)
        gather_stats(g)
        if early:

            @pl.when(column == 0)
            def _():
                hidden_send[a0] = hidden[g].astype(bf16)
                for k in range(tp - 1):
                    ship(2, k, a0).start()

    def first_loads():
        loads[1].wait()
        loads[2].wait()
        proj_all[...] = (
            lax.dot_general(
                context[...],
                in_table[...].astype(f32).astype(bf16),
                (((1,), (1,)), ((), ())),
                preferred_element_type=f32,
            )
            * in_scale
        ).astype(bf16)
        for k in range(tp - 1):
            send_proj(k).start()
        for copy in loads[3:]:
            copy.wait()
        if early:

            @pl.loop(0, lines)
            def _(j):
                for k in range(tp - 1):
                    ship(0, k, j).start()
                    ship(1, k, j).start()

    for h in (1, 0):
        pass_on(h, a, jnp.int32(0))
    first_loads()

    @pl.loop(1, lines + 3)
    def _(s):
        if group == 2:

            @pl.loop(0, 4)
            def _(e):
                event(e, s - 1, chip_forward)

            @pl.loop(0, 4)
            def _(e):
                event(e, s - 2, chip_stats)

        else:

            @pl.loop(0, 4)
            def _(e):
                event(e, s - 1, whole_chip)

        for h in (1, 0):

            @pl.loop(0, 4)
            def _(e):
                event(e, s, functools.partial(pass_on, h))

    if group != 2:

        @pl.loop(0, groups)
        def _(g):
            forward(g)

        @pl.loop(0, groups)
        def _(g):
            gather_stats(g)

    rstd = lax.rsqrt(square[...] * (1.0 / width) + epsilon)
    pull = rstd * rstd * rstd * (cross[...] * (1.0 / width))
    square[...] = rstd
    cross[...] = pull
    if early:
        lane = lax.broadcasted_iota(jnp.int32, (rows, 128), 1)
        stat_send[...] = jnp.where(lane < 64, rstd, pull)
        for k in range(tp - 1):
            send_stat(k).start()

    def send_gh(k, g):
        return pltpu.make_async_remote_copy(
            src_ref=gh_all.at[t, g],
            dst_ref=gh_all.at[t, g],
            send_sem=gh_send.at[k, g],
            recv_sem=gh_recv.at[tp - 2 - k, g],
            device_id=(me, peer(k)),
            device_id_type=MESH,
        )

    def await_gh(k, g):
        pltpu.make_async_remote_copy(
            src_ref=gh_all.at[peer(k), g],
            dst_ref=gh_all.at[peer(k), g],
            send_sem=gh_send.at[k, g],
            recv_sem=gh_recv.at[k, g],
            device_id=(me, peer(k)),
            device_id_type=MESH,
        ).wait_recv()

    def own_grad(g):
        value = (
            stream[:, block(g)].astype(f32)
            + square[...] * weighted_of(g)
            - hidden[g] * cross[...]
        ).astype(bf16)
        gh_all[t, g] = value
        gh_out[:, block(g)] = value

    def sent(act):
        @pl.loop(0, lines if early else groups)
        def _(j):
            act(2 * j + 1 - b if early else j)

    def own_and_send(g):
        own_grad(g)
        for k in range(tp - 1):
            send_gh(k, g).start()

    sent(own_and_send)
    if early:

        @pl.loop(0, lines)
        def _(j):
            own_grad(2 * j + b)

    out_proj = (
        lax.dot_general(
            gh_out[...],
            out_table[...].astype(f32).astype(bf16),
            (((1,), (1,)), ((), ())),
            preferred_element_type=f32,
        )
        * out_scale
    )
    in_proj = proj_all[own_rows, :].astype(f32)
    for k in range(tp - 1):
        send_proj(k).wait_recv()
    for k in range(tp - 1):
        in_proj = in_proj + proj_in[k].astype(f32)
    sk_all[...] = lax.dot_general(
        in_proj,
        out_proj,
        (((0,), (0,)), ((), ())),
        precision=lax.Precision.HIGHEST,
        preferred_element_type=f32,
    )
    piece = sk_out.shape[0]

    def send_skt(k):
        return pltpu.make_async_remote_copy(
            src_ref=sk_all.at[pl.ds(pl.multiple_of(peer(k) * piece, piece), piece)],
            dst_ref=sk_tensor.at[tp - 2 - k],
            send_sem=skt_send.at[k],
            recv_sem=skt_recv.at[tp - 2 - k],
            device_id=(me, peer(k)),
            device_id_type=MESH,
        )

    for k in range(tp - 1):
        send_skt(k).start()

    def add(row, g):
        total[...] += jnp.dot(gh_all[row, g], weight[block(g), :], preferred_element_type=f32)

    def finish(row):
        gc_out[pl.ds(pl.multiple_of(row * rows, rows), rows), :] = total[...].astype(bf16)

    total[...] = jnp.zeros_like(total)

    @pl.loop(0, groups)
    def _(g):
        add(t, g)

    finish(t)

    summed = sk_all[pl.ds(pl.multiple_of(t * piece, piece), piece), :]
    for k in range(tp - 1):
        send_skt(k).wait_recv()
    for k in range(tp - 1):
        summed = summed + sk_tensor[k]
    summed = summed * (1.0 / math.sqrt(context.shape[0]))
    sk_out[...] = summed

    def send_skd(r):
        return pltpu.make_async_remote_copy(
            src_ref=sk_send.at[r],
            dst_ref=sk_in.at[me],
            send_sem=skd_send.at[r],
            recv_sem=skd_recv.at[me],
            device_id=(r, t),
            device_id_type=MESH,
        )

    def await_skd(r):
        pltpu.make_async_remote_copy(
            src_ref=sk_in.at[r],
            dst_ref=sk_in.at[r],
            send_sem=skd_send.at[r],
            recv_sem=skd_recv.at[r],
            device_id=(r, t),
            device_id_type=MESH,
        ).wait_recv()

    owner = jnp.broadcast_to(ids_ref[0:1, 0:1], sk_out.shape)

    @pl.loop(1, dp)
    def _(k):
        r = lax.rem(me + k, dp)
        sk_send[r] = jnp.where(owner == r, sk_out[...], 0.0)
        send_skd(r).start()

    for k in range(tp - 1):
        total[...] = jnp.zeros_like(total)
        if early:
            send_stat(tp - 2 - k).wait_recv()

            @pl.loop(0, lines)
            def _(j):
                g = 2 * j + b
                for n in range(3):
                    await_ship(n, k, j)
                gh_all[peer(k), g] = (
                    early_stream[k, j].astype(f32)
                    + stat_in[k, :, 0:1] * (gain_ref[:, block(g)] * early_normed[k, j].astype(f32))
                    - early_hidden[k, j].astype(f32) * stat_in[k, :, 64:65]
                ).astype(bf16)
                add(peer(k), g)

        def arrived(g):
            await_gh(k, g)
            add(peer(k), g)

        sent(arrived)
        finish(peer(k))

    sk_out[...] = jnp.where(owner == me, sk_out[...], 0.0)

    @pl.loop(1, dp)
    def _(k):
        r = lax.rem(me + k, dp)
        await_skd(r)
        sk_out[...] += sk_in[r]

    @pl.loop(0, lines)
    def _(a0):
        for column in (0, 1):
            for h in (1, 0):
                ways(a0, jnp.int32(column), h, lambda copy: copy.wait_send())

    for k in range(tp - 1):
        send_proj(k).wait_send()
        send_skt(k).wait_send()

        @pl.loop(0, groups)
        def _(g):
            send_part(k, g).wait_send()

        sent(lambda g: send_gh(k, g).wait_send())
        if early:
            send_stat(k).wait_send()

            @pl.loop(0, lines)
            def _(j):
                for n in range(3):
                    ship(n, k, j).wait_send()

    @pl.loop(1, dp)
    def _(k):
        send_skd(lax.rem(me + k, dp)).wait_send()


def on_device(
    context,
    residual,
    out_weight,
    norm_gain,
    normed_grad,
    stream_grad,
    sketch_in,
    sketch_out,
    example_ids,
):
    tp = lax.axis_size("tensor")
    dp = lax.axis_size("dp")
    tokens, heads = context.shape
    rows, width = residual.shape
    shard = out_weight.shape[0]
    rank = sketch_in.shape[1]
    group = 2
    while (group * shard) % 128:
        group *= 2
    cols = group * shard
    groups = width // cols
    early = (dp // 4, rows, cols) if group == 2 else (1, 16, 128)
    piece = rank // tp
    hbm = pl.BlockSpec(memory_space=pl.ANY)
    vmem = pl.BlockSpec(memory_space=pltpu.VMEM)
    dma = pltpu.SemaphoreType.DMA
    flops = 4 * tokens * heads * width
    grad_hidden, grad_context, sketch = pl.pallas_call(
        functools.partial(kernel, dp, tp, group),
        out_shape=(
            jax.ShapeDtypeStruct((rows, width), bf16),
            jax.ShapeDtypeStruct((tokens, heads), bf16),
            jax.ShapeDtypeStruct((piece, rank), f32),
        ),
        in_specs=[hbm, hbm, hbm, vmem, hbm, hbm, hbm, hbm, vmem],
        out_specs=(vmem, vmem, vmem),
        scratch_shapes=[
            pltpu.VMEM((width, heads), bf16),
            pltpu.VMEM((tokens, heads), bf16),
            pltpu.VMEM((rows, width), bf16),
            pltpu.VMEM((rows, width), bf16),
            pltpu.VMEM((rows, width), bf16),
            pltpu.VMEM((rank, heads), jnp.int32),
            pltpu.VMEM((rank, width), jnp.int32),
            pltpu.VMEM((groups, tokens, cols), bf16),
            pltpu.VMEM((tp - 1, groups, rows, cols), bf16),
            pltpu.VMEM((groups, rows, cols), f32),
            pltpu.VMEM((rows, 1), f32),
            pltpu.VMEM((rows, 1), f32),
            pltpu.VMEM((tp, groups, rows, cols), bf16),
            pltpu.VMEM((rows, heads), f32),
            pltpu.VMEM((tokens, rank), bf16),
            pltpu.VMEM((tp - 1, rows, rank), bf16),
            pltpu.VMEM((rank, rank), f32),
            pltpu.VMEM((tp - 1, piece, rank), f32),
            pltpu.VMEM((dp, piece, rank), f32),
            pltpu.VMEM((dp, piece, rank), f32),
            dma((7,)),
            dma((4, 2, dp)),
            dma((2, dp)),
            dma((tp - 1, groups)),
            dma((tp - 1, groups)),
            dma((tp - 1, groups)),
            dma((tp - 1, groups)),
            dma((tp - 1,)),
            dma((tp - 1,)),
            dma((tp - 1,)),
            dma((tp - 1,)),
            dma((dp,)),
            dma((dp,)),
            pltpu.VMEM((tp - 1,) + early, bf16),
            pltpu.VMEM((tp - 1,) + early, bf16),
            pltpu.VMEM((tp - 1,) + early, bf16),
            pltpu.VMEM(early, bf16),
            pltpu.VMEM((rows, 128), f32),
            pltpu.VMEM((tp - 1, rows, 128), f32),
            dma((3, tp - 1, early[0])),
            dma((3, tp - 1, early[0])),
            dma((tp - 1,)),
            dma((tp - 1,)),
        ],
        compiler_params=pltpu.CompilerParams(
            collective_id=0, has_side_effects=True, vmem_limit_bytes=56 * 1024 * 1024
        ),
        cost_estimate=pl.CostEstimate(
            flops=flops, bytes_accessed=16 * 1024 * 1024, transcendentals=0
        ),
    )(
        context,
        residual,
        out_weight,
        norm_gain.reshape(1, width),
        normed_grad,
        stream_grad,
        sketch_in.T,
        sketch_out.T,
        example_ids.reshape(1, rows),
    )
    return (grad_hidden, grad_context, sketch.reshape(1, piece * rank))


def solution(mesh):
    return jax.shard_map(
        on_device,
        mesh=mesh,
        in_specs=(
            P("dp", "tensor"),
            P(("dp", "tensor"), None),
            P("dp", "tensor"),
            P(),
            P(("dp", "tensor"), None),
            P(("dp", "tensor"), None),
            P("tensor", None),
            P(),
            P(("dp", "tensor")),
        ),
        out_specs=(P(("dp", "tensor"), None), P("dp", "tensor"), P("dp", "tensor")),
        check_vma=False,
    )
```
